128 devices in a mesh: row: 4 (over z_hi, core), col: 32 (over z_lo, x, y).
Axes of the slice: x: 4, y: 4, z: 4 (z_hi: 2, z_lo: 2; z = z_hi * 2 + z_lo), core: 2. Of those that a mesh axis runs over, the one named last changes fastest.
Arguments:
- weight: bfloat16 [12288, 53248], P('row', 'col'), may hold values from -6 to 6
- sketch: bfloat16 [53248, 64], P('col'), may hold values from -6 to 6
- codebook: bfloat16 [16], replicated, may hold values from -1 to 1, as said below
Outputs:
- quant_weight: bfloat16 [12288, 53248], P(('row', 'col'))
- block_scales: float32 [12288, 832], P(('row', 'col'))
- lora_a: float32 [12288, 64], P('row')
- lora_b: float32 [64, 53248], P(None, 'col')
The draws below stay inside these ranges and needn't reach their ends.
Inputs may be any that keep to these rules, and one draw needn't show every extreme that they name: `codebook`: strictly increasing, first entry -1 and last entry 1.
All inputs are finite; a program needn't handle non-finite values.
Results may differ from the reference program's by a relative error of at most 0.013.
Values may be sent and summed in bfloat16 or wider, within the bound.
A program may use at most 192 MiB of HBM per device.

```python
import math
import jax
import jax.numpy as jnp
from jax import lax

ROWS = 12288
COLS = 53248
RANK = 64
BLOCK = 64
POWER = 2
LEVELS = 16


def draw_codebook(key, part):
    key = jax.random.fold_in(key, 7)
    gaps = jax.random.uniform(key, (LEVELS - 1,), jnp.float32, 0.3, 1.7)
    total = jnp.cumsum(gaps)
    levels = jnp.concatenate([jnp.zeros((1,), jnp.float32), total]) / total[-1] * 2.0 - 1.0
    levels = levels.at[0].set(-1.0).at[LEVELS - 1].set(1.0)
    return levels.astype(jnp.bfloat16)


def block_scale(own_key, extent, split, smallest, top_value):
    level, own = 1.0, jax.random.fold_in(own_key, 6)
    for position, blocks in split:
        steps = jnp.exp(jax.random.uniform(jax.random.fold_in(own, position), (blocks,), jnp.float32, smallest / len(split), top_value / len(split)))
        level = level * jnp.repeat(steps, extent[position] // blocks).reshape([-1 if axis == position else 1 for axis in range(len(extent))])
    return level


def scatter_about(stream_key, shape, deviation, reach, cuts=(), held_as=jnp.bfloat16):
    factor_of = block_scale(stream_key, shape, cuts, -0.22, 0.18) if cuts else 1.0
    result = jax.random.normal(stream_key, shape, jnp.float32) * deviation * factor_of
    return jnp.minimum(jnp.maximum(result, -reach), reach).astype(held_as)


def setup_inputs(seed: int = 0) -> dict:
    key_of = jax.random.split(jax.random.key(seed), 4)
    return {
        "weight": scatter_about(key_of[0], (ROWS, COLS), 1.0, 6.0, ((0, 4), (1, 32))),
        "sketch": scatter_about(key_of[1], (COLS, RANK), 1.0, 6.0, ((0, 32),)),
        "codebook": draw_codebook(jax.random.fold_in(key_of[3], 71), 0),
    }


def quantize(block_rows, codebook):
    rows, cols = block_rows.shape
    values = block_rows.astype(jnp.float32)
    scales = lax.optimization_barrier(jnp.max(jnp.abs(values.reshape(rows, cols // BLOCK, BLOCK)), axis=2))
    spread = jnp.repeat(scales, BLOCK, axis=1)
    levels = codebook.astype(jnp.float32)
    middles = (levels[:-1] + levels[1:]) * 0.5
    jumps = levels[1:] - levels[:-1]
    level = jnp.zeros_like(values) + levels[0]
    for index in range(LEVELS - 1):
        level = level + jnp.where(values > middles[index] * spread, jumps[index], 0.0)
    return (level * spread, scales)

def orthonormal(sample):
    gram = jnp.dot(sample.T.astype(jnp.float32), sample.astype(jnp.float32), precision=lax.Precision.HIGHEST, preferred_element_type=jnp.float32)
    lower = jnp.linalg.cholesky(gram)
    return jax.scipy.linalg.solve_triangular(lower, sample.T, lower=True).T

def reference(weight, sketch, codebook):
    height = math.gcd(ROWS, 1024)
    pieces = weight.reshape(ROWS // height, height, COLS)

    def one_piece(piece):
        dequant, scales = quantize(piece, codebook)
        return (dequant.astype(jnp.bfloat16), scales, piece.astype(jnp.float32) - dequant)
    quant_weight, block_scales, residual = lax.map(one_piece, pieces)
    quant_weight = quant_weight.reshape(ROWS, COLS)
    block_scales = block_scales.reshape(ROWS, COLS // BLOCK)
    residual = residual.reshape(ROWS, COLS)
    high = lax.Precision.HIGHEST
    basis = orthonormal(jnp.dot(residual.astype(jnp.float32), sketch.astype(jnp.float32), precision=high, preferred_element_type=jnp.float32))
    for step in range(POWER):
        project = jnp.dot(residual.T.astype(jnp.float32), basis.astype(jnp.float32), precision=high, preferred_element_type=jnp.float32)
        basis = orthonormal(jnp.dot(residual.astype(jnp.float32), project.astype(jnp.float32), precision=high, preferred_element_type=jnp.float32))
    project = jnp.dot(residual.T.astype(jnp.float32), basis.astype(jnp.float32), precision=high, preferred_element_type=jnp.float32)
    factor = math.sqrt(ROWS)
    return (quant_weight, block_scales, basis * factor, project.T / factor)
```

```python
import functools
import math

import jax
import jax.numpy as jnp
from jax import lax
from jax.experimental import pallas as pl
from jax.experimental.pallas import tpu as pltpu
from jax.sharding import PartitionSpec as P

ROWS = 12288
BLOCK = 64
POWER = 2
LEVELS = 16
RANK = 64
NCOL = 32
HIGH = lax.Precision.HIGHEST
MESH = pl.DeviceIdType.MESH
F32 = jnp.float32
BF16 = jnp.bfloat16

ROUNDS = (
    ((1, 1, 0), (3, 3, 1)),
    ((2, 0, 0), (0, 2, 1)),
    ((1, 3, 0), (3, 1, 1)),
    ((2, 1, 0), (0, 3, 1)),
    ((1, 2, 0), (3, 0, 1)),
    ((2, 2, 1),),
    ((1, 1, 1), (3, 3, 0)),
    ((2, 3, 0), (0, 1, 1)),
    ((3, 2, 0), (1, 0, 1)),
    ((2, 0, 1), (0, 2, 0)),
    ((1, 3, 1), (3, 1, 0)),
    ((2, 1, 1), (0, 3, 0)),
    ((1, 2, 1), (3, 0, 0)),
    ((2, 3, 1), (0, 1, 0)),
    ((3, 2, 1), (1, 0, 0)),
    ((2, 2, 0), (0, 0, 1)),
)
CODES = tuple(dx + 4 * dy + 16 * dz for group in ROUNDS for dx, dy, dz in group)
EARLY = 8
PACE = (2, 2, 2, 1, 1, 2, 2, 2, 1, 1, 2, 2, 1, 1, 1)


def partner(me, code):
    x, y, z = (me // 4) % 4, me % 4, me // 16
    dx, dy, dz = code % 4, (code // 4) % 4, code // 16
    return (z + dz) % 2 * 16 + (x + dx) % 4 * 4 + (y + dy) % 4


def code_at(index):
    code = 0
    for place, value in enumerate(CODES):
        code = jnp.where(index == place, value, code)
    return code


def dot(a, b, precision=None):
    return lax.dot_general(a, b, (((1,), (0,)), ((), ())), precision=precision, preferred_element_type=F32)


def dot_nt(a, b, precision=None):
    return lax.dot_general(a, b, (((1,), (1,)), ((), ())), precision=precision, preferred_element_type=F32)


def drain(ref, sem):
    pltpu.make_async_copy(ref, ref, sem).wait()


def kernel(
    weight, sketch, codebook,
    quant, scales, lora_a, lora_b,
    deq, res, scale_out, factor_top, factor_bot, sample_out, reduce_in, gather_in, sample_t,
    project, half_in, pair_in, total, gram_in, gram_out, work,
    load_sem, block_sem, scale_sem, own_sem, reduce_sem, gather_sem, half_sem, pair_sem, total_sem, gram_sem,
):
    cols = deq.shape[2]
    tiles = cols // 128
    per_block = deq.shape[1]
    half = per_block // 2
    row, me = lax.axis_index("row"), lax.axis_index("col")
    core = row % 2
    mate = row + 1 - 2 * core
    across = (row + 2) % 4
    peers = [partner(me, code) for code in CODES]

    def load(index):
        return pltpu.make_async_copy(
            weight.at[pl.ds(pl.multiple_of(index * per_block, per_block), per_block), :], deq.at[index], load_sem.at[index]
        )

    def start_load(index, carry):
        load(partner(me, code_at(index))).start()
        return carry

    lax.fori_loop(0, NCOL, start_load, 0)

    barrier = pltpu.get_barrier_semaphore()
    for peer in peers:
        pl.semaphore_signal(barrier, inc=1, device_id=(row, peer), device_id_type=MESH)
    for other in (1, 2, 3):
        pl.semaphore_signal(barrier, inc=1, device_id=((row + other) % 4, me), device_id_type=MESH)

    unit = (lax.broadcasted_iota(jnp.int32, (RANK, RANK), 0) == lax.broadcasted_iota(jnp.int32, (RANK, RANK), 1))
    factor_top[...] = jnp.zeros(factor_top.shape, BF16)
    factor_bot[...] = jnp.zeros(factor_bot.shape, BF16)
    turned = dot_nt(unit.astype(BF16), sketch[...]).astype(BF16)
    factor_top[0:RANK, :] = turned
    factor_bot[RANK : 2 * RANK, :] = turned

    levels = [codebook[k] for k in range(LEVELS)]
    middles = []
    for k in range(LEVELS - 1):
        middle = (levels[k] + levels[k + 1]) * 0.5
        middles.append(middle + jnp.abs(middle) * 2.0**-21)

    pl.semaphore_wait(barrier, len(peers) + 3)

    def send_block(place, peer):
        blocks = pltpu.make_async_remote_copy(
            src_ref=deq.at[peer], dst_ref=quant.at[:, pl.ds(pl.multiple_of(me * cols, 128), cols)],
            send_sem=block_sem.at[0], recv_sem=block_sem.at[1], device_id=(row, peer), device_id_type=MESH,
        )
        blocks.start()
        pltpu.make_async_remote_copy(
            src_ref=scale_out.at[peer], dst_ref=scales.at[me],
            send_sem=scale_sem.at[0], recv_sem=scale_sem.at[1], device_id=(row, peer), device_id_type=MESH,
        ).start()

    lane = lax.broadcasted_iota(jnp.int32, (16, 128), 1)

    def quantize_block(place, carry):
        block = partner(me, code_at(place))
        load(block).wait()

        def quantize_rows(group, inner):
            rows = pl.ds(pl.multiple_of(group * 16, 16), 16)
            shift = group // 2 * 32
            gathered = jnp.zeros((16, 128), F32)
            for tile in range(tiles):
                columns = slice(tile * 128, tile * 128 + 128)
                value = deq[block, rows, columns].astype(F32)
                size = jnp.abs(value)
                left = jnp.max(jnp.where(lane < BLOCK, size, 0.0), axis=1, keepdims=True)
                right = jnp.max(jnp.where(lane < BLOCK, 0.0, size), axis=1, keepdims=True)
                gathered = jnp.where(lane == shift + 2 * tile, left, gathered)
                gathered = jnp.where(lane == shift + 2 * tile + 1, right, gathered)
                spread = jnp.where(lane < BLOCK, left, right)
                unit_value = value * (1.0 / spread)
                level = jnp.full((16, 128), levels[0], F32)
                for k in range(LEVELS - 1):
                    level = jnp.where(unit_value > middles[k], levels[k + 1], level)
                dequant = level * spread
                deq[block, rows, columns] = dequant.astype(BF16)
                res[block, group // 3, pl.ds(pl.multiple_of(group % 3 * 16, 16), 16), columns] = (value - dequant).astype(BF16)
            held = pl.ds(pl.multiple_of(group % 2 * 16, 16), 16)
            before = scale_out[block, held, :].astype(F32)
            scale_out[block, held, :] = jnp.where(lane < shift, before, gathered).astype(BF16)
            return inner

        lax.fori_loop(0, per_block // 16, quantize_rows, 0)

        @pl.when(place < EARLY)
        def _():
            send_block(place, block)

        return carry

    scale_out[...] = jnp.zeros(scale_out.shape, BF16)
    lax.fori_loop(0, NCOL, quantize_block, 0)

    own = [
        pltpu.make_async_copy(deq.at[me], quant.at[:, pl.ds(pl.multiple_of(me * cols, 128), cols)], own_sem.at[0]),
        pltpu.make_async_copy(scale_out.at[me], scales.at[me], own_sem.at[1]),
    ]

    state = {"sent": EARLY, "point": 0}

    def breathe(last=False):
        count = len(CODES) if last else PACE[state["point"]]
        state["point"] += 1
        for place in range(state["sent"], min(state["sent"] + count, len(CODES))):
            send_block(place, peers[place])
            state["sent"] = place + 1

    def sample(step):
        def some(part, carry):
            blocks = pl.ds(pl.multiple_of(part * 8, 8), 8)
            top = res[blocks, 0].reshape(8 * half, cols)
            bottom = res[blocks, 1].reshape(8 * half, cols)
            both = dot_nt(top, factor_top[...]) + dot_nt(bottom, factor_bot[...])
            both = both[:, 0:128] + both[:, 128:256]
            sample_out[blocks] = both.reshape(8, half, 128).astype(BF16)
            return carry

        lax.fori_loop(0, NCOL // 8, some, 0)
        reduce_in[step, pl.ds(me, 1)] = sample_out[pl.ds(me, 1)]
        for peer in peers:
            pltpu.make_async_remote_copy(
                src_ref=sample_out.at[peer], dst_ref=reduce_in.at[step, me],
                send_sem=reduce_sem.at[step, 0], recv_sem=reduce_sem.at[step, 1], device_id=(row, peer), device_id_type=MESH,
            ).start()
        breathe()
        drain(reduce_in.at[step, 0 : NCOL - 1], reduce_sem.at[step, 1])
        mine = jnp.sum(reduce_in[step].astype(F32), axis=0)
        gather_in[step, pl.ds(me, 1)] = mine.astype(BF16)[None]
        for peer in peers:
            pltpu.make_async_remote_copy(
                src_ref=gather_in.at[step, me], dst_ref=gather_in.at[step, me],
                send_sem=gather_sem.at[step, 0], recv_sem=gather_sem.at[step, 1], device_id=(row, peer), device_id_type=MESH,
            ).start()
        breathe()
        drain(reduce_in.at[step, 0 : NCOL - 1], reduce_sem.at[step, 0])
        drain(gather_in.at[step, 0 : NCOL - 1], gather_sem.at[step, 1])

    def begin_gram(step):
        packed = gather_in[step].reshape(NCOL * half, 128)
        sample_t[...] = packed.astype(F32).T.astype(BF16)
        gram = dot(sample_t[...], packed)
        gram = gram[0:RANK] + pltpu.roll(gram[RANK : 2 * RANK], RANK, 1)
        gram_out[step] = gram
        gram_in[step, pl.ds(row, 1)] = gram[None]
        for other in (1, 2, 3):
            pltpu.make_async_remote_copy(
                src_ref=gram_out.at[step], dst_ref=gram_in.at[step, row],
                send_sem=gram_sem.at[step, 0], recv_sem=gram_sem.at[step, 1],
                device_id=((row + other) % 4, me), device_id_type=MESH,
            ).start()

    def end_gram(step):
        drain(gram_in.at[step, 0:3], gram_sem.at[step, 1])
        drain(gram_in.at[step, 0:3], gram_sem.at[step, 0])
        gram = (gram_in[step, 0] + gram_in[step, 1]) + (gram_in[step, 2] + gram_in[step, 3])
        lanes = lax.broadcasted_iota(jnp.int32, (RANK, 128), 1)
        subs = lax.broadcasted_iota(jnp.int32, (RANK, 128), 0)
        work[...] = jnp.where(lanes < RANK, gram, jnp.where(lanes - RANK == subs, 1.0, 0.0))

    def eliminate(first, last):
        lanes = lax.broadcasted_iota(jnp.int32, (RANK, 128), 1)
        subs = lax.broadcasted_iota(jnp.int32, (RANK, 1), 0)

        def pivot(k, carry):
            held = work[...]
            line = work[pl.ds(k, 1), :]
            column = jnp.sum(jnp.where(lanes == k, held, 0.0), axis=1, keepdims=True)
            top = jnp.sum(jnp.where(lanes[0:1] == k, line, 0.0), axis=1, keepdims=True)
            scaled = jnp.where(subs > k, column, 0.0) * (1.0 / top)
            work[...] = held - scaled * line
            return carry

        lax.fori_loop(first, last, pivot, 0)

    def inverse_factor():
        lanes = lax.broadcasted_iota(jnp.int32, (RANK, 128), 1)
        subs = lax.broadcasted_iota(jnp.int32, (RANK, 128), 0)
        held = work[...]
        pivots = jnp.sum(jnp.where(lanes == subs, held, 0.0), axis=1, keepdims=True)
        return jnp.where(lanes < RANK, 0.0, held * (1.0 / jnp.sqrt(pivots)))

    def project_all(step):
        project[...] = jnp.zeros(project.shape, F32)

        def some(part, carry):
            blocks = pl.ds(pl.multiple_of(part * 16, 16), 16)
            depth = pl.ds(pl.multiple_of(part * 16 * half, 128), 16 * half)
            top = res[blocks, 0].reshape(16 * half, cols)
            bottom = res[blocks, 1].reshape(16 * half, cols)
            project[...] += dot(sample_t[0:RANK, depth], top) + dot(sample_t[RANK : 2 * RANK, depth], bottom)
            return carry

        lax.fori_loop(0, NCOL // 16, some, 0)

    def reduce_project(step):
        part = RANK // 2
        mine = pl.ds(pl.multiple_of(core * part, part), part)
        other = pl.ds(pl.multiple_of((1 - core) * part, part), part)
        one = pltpu.make_async_remote_copy(
            src_ref=project.at[other, :], dst_ref=half_in.at[step],
            send_sem=half_sem.at[step, 0], recv_sem=half_sem.at[step, 1], device_id=(mate, me), device_id_type=MESH,
        )
        one.start()
        breathe()
        end_gram(step)
        one.wait()
        project[mine, :] = project[mine, :] + half_in[step]
        two = pltpu.make_async_remote_copy(
            src_ref=project.at[mine, :], dst_ref=pair_in.at[step],
            send_sem=pair_sem.at[step, 0], recv_sem=pair_sem.at[step, 1], device_id=(across, me), device_id_type=MESH,
        )
        two.start()
        breathe()
        eliminate(0, RANK // 2)
        two.wait()
        total[step, mine, :] = project[mine, :] + pair_in[step]
        three = pltpu.make_async_remote_copy(
            src_ref=total.at[step, mine, :], dst_ref=total.at[step, mine, :],
            send_sem=total_sem.at[step, 0], recv_sem=total_sem.at[step, 1], device_id=(mate, me), device_id_type=MESH,
        )
        three.start()
        breathe()
        eliminate(RANK // 2, RANK)
        three.wait()

    root = math.sqrt(ROWS)
    for step in range(POWER + 1):
        sample(step)
        if step == 0:
            for copy in own:
                copy.start()
        begin_gram(step)
        project_all(step)
        reduce_project(step)
        inverse = inverse_factor()
        factor = dot(pltpu.roll(inverse, RANK, 1)[:, 0:RANK], total[step], HIGH)
        if step < POWER:
            upper = factor.astype(BF16)
            lower = (factor - upper.astype(F32)).astype(BF16)
            factor_top[0:RANK, :] = upper
            factor_top[2 * RANK : 3 * RANK, :] = lower
            factor_bot[RANK : 2 * RANK, :] = upper
            factor_bot[3 * RANK : 4 * RANK, :] = lower
        else:
            lora_b[...] = factor * (1.0 / root)
            packed = gather_in[step].reshape(NCOL * half, 128).astype(F32)
            right = inverse * root
            left = pltpu.roll(right, RANK, 1)
            lora_a[:, 0] = dot_nt(packed, left, HIGH).reshape(NCOL, half, RANK)
            lora_a[:, 1] = dot_nt(packed, right, HIGH).reshape(NCOL, half, RANK)
        drain(gather_in.at[step, 0 : NCOL - 1], gather_sem.at[step, 0])
    breathe(last=True)

    for copy in own:
        copy.wait()
    drain(scale_out.at[0 : NCOL - 1], scale_sem.at[0])
    drain(scales.at[0 : NCOL - 1], scale_sem.at[1])
    drain(deq.at[0 : NCOL - 1], block_sem.at[0])
    drain(quant.at[:, pl.ds(0, (NCOL - 1) * cols)], block_sem.at[1])


def body(weight, sketch, codebook):
    rows, cols = weight.shape
    per_block = rows // NCOL
    half = per_block // 2
    steps = POWER + 1
    anywhere = pl.BlockSpec(memory_space=pl.ANY)
    local = pl.BlockSpec(memory_space=pltpu.VMEM)
    dma = pltpu.SemaphoreType.DMA
    quant, scales, lora_a, lora_b = pl.pallas_call(
        kernel,
        name="loftq",
        out_shape=(
            jax.ShapeDtypeStruct((per_block, NCOL * cols), BF16),
            jax.ShapeDtypeStruct((NCOL, 32, 128), BF16),
            jax.ShapeDtypeStruct((NCOL, 2, half, RANK), F32),
            jax.ShapeDtypeStruct((RANK, cols), F32),
        ),
        in_specs=[anywhere, local, pl.BlockSpec(memory_space=pltpu.SMEM)],
        out_specs=(anywhere, anywhere, local, local),
        scratch_shapes=[
            pltpu.VMEM((NCOL, per_block, cols), BF16),
            pltpu.VMEM((NCOL, 2, half, cols), BF16),
            pltpu.VMEM((NCOL, 32, 128), BF16),
            pltpu.VMEM((4 * RANK, cols), BF16),
            pltpu.VMEM((4 * RANK, cols), BF16),
            pltpu.VMEM((NCOL, half, 128), BF16),
            pltpu.VMEM((steps, NCOL, half, 128), BF16),
            pltpu.VMEM((steps, NCOL, half, 128), BF16),
            pltpu.VMEM((128, NCOL * half), BF16),
            pltpu.VMEM((RANK, cols), F32),
            pltpu.VMEM((steps, RANK // 2, cols), F32),
            pltpu.VMEM((steps, RANK // 2, cols), F32),
            pltpu.VMEM((steps, RANK, cols), F32),
            pltpu.VMEM((steps, 4, RANK, 128), F32),
            pltpu.VMEM((steps, RANK, 128), F32),
            pltpu.VMEM((RANK, 128), F32),
            dma((NCOL,)),
            dma((2,)),
            dma((2,)),
            dma((2,)),
            dma((steps, 2)),
            dma((steps, 2)),
            dma((steps, 2)),
            dma((steps, 2)),
            dma((steps, 2)),
            dma((steps, 2)),
        ],
        compiler_params=pltpu.CompilerParams(
            collective_id=0, has_side_effects=True, vmem_limit_bytes=56 * 1024 * 1024
        ),
    )(weight, sketch, codebook.astype(F32))
    blocks = cols // BLOCK
    scales = scales[:, :, :96].reshape(NCOL, 32, 3, 32)[..., :blocks]
    scales = scales.transpose(2, 1, 0, 3).reshape(per_block, NCOL * blocks).astype(F32)
    return quant, scales, lora_a.reshape(rows, RANK), lora_b


def solution(mesh):
    in_specs = (P("row", "col"), P("col", None), P())
    out_specs = (P(("row", "col"), None), P(("row", "col"), None), P("row", None), P(None, "col"))
    return jax.shard_map(body, mesh=mesh, in_specs=in_specs, out_specs=out_specs, check_vma=False)
```

```python
import functools
import math

import jax
import jax.numpy as jnp
from jax import lax
from jax.experimental import pallas as pl
from jax.experimental.pallas import tpu as pltpu
from jax.sharding import PartitionSpec as P

ROWS = 12288
BLOCK = 64
POWER = 2
LEVELS = 16
RANK = 64
NCOL = 32
HIGH = lax.Precision.HIGHEST
MESH = pl.DeviceIdType.MESH
F32 = jnp.float32
BF16 = jnp.bfloat16

ROUNDS = (
    ((1, 1, 0), (3, 3, 1)),
    ((1, 1, 1), (3, 3, 0)),
    ((1, 3, 0), (3, 1, 1)),
    ((1, 3, 1), (3, 1, 0)),
    ((2, 0, 0), (0, 2, 1)),
    ((2, 0, 1), (0, 2, 0)),
    ((2, 1, 0), (0, 3, 1)),
    ((2, 1, 1), (0, 3, 0)),
    ((2, 3, 0), (0, 1, 1)),
    ((2, 3, 1), (0, 1, 0)),
    ((1, 2, 0), (3, 0, 1)),
    ((1, 2, 1), (3, 0, 0)),
    ((3, 2, 0), (1, 0, 1)),
    ((3, 2, 1), (1, 0, 0)),
    ((2, 2, 1),),
    ((2, 2, 0), (0, 0, 1)),
)
CODES = tuple(dx + 4 * dy + 16 * dz for group in ROUNDS for dx, dy, dz in group)
EARLY = 6
SPACING = 5
CUTS = 3
PACE = (0, 0, 0, 1, 0, 0, 2) + (1, 0, 0, 1, 0, 0, 2) * 2
WINDOW = 6


def partner(me, code):
    x, y, z = (me // 4) % 4, me % 4, me // 16
    dx, dy, dz = code % 4, (code // 4) % 4, code // 16
    return (z + dz) % 2 * 16 + (x + dx) % 4 * 4 + (y + dy) % 4


def code_at(index):
    code = 0
    for place, value in enumerate(CODES):
        code = jnp.where(index == place, value, code)
    return code


def dot(a, b, precision=None):
    return lax.dot_general(a, b, (((1,), (0,)), ((), ())), precision=precision, preferred_element_type=F32)


def dot_nt(a, b, precision=None):
    return lax.dot_general(a, b, (((1,), (1,)), ((), ())), precision=precision, preferred_element_type=F32)


def drain(ref, sem):
    pltpu.make_async_copy(ref, ref, sem).wait()


def kernel(
    weight, sketch, codebook,
    quant, scales, lora_a, lora_b,
    deq, res, scale_out, factor_top, factor_bot, sample_out, reduce_in, gather_in, sample_t,
    project, half_in, pair_out, pair_in, last_out, last_in, total, gram_in, gram_out, work,
    load_sem, block_sem, scale_sem, own_sem, reduce_sem, gather_sem, half_sem, pair_sem, total_sem, gram_sem, tail_sem,
):
    cols = deq.shape[2]
    tiles = cols // 128
    per_block = deq.shape[1]
    half = per_block // 2
    row, me = lax.axis_index("row"), lax.axis_index("col")
    core = row % 2
    mate = row + 1 - 2 * core
    across = (row + 2) % 4
    peers = [partner(me, code) for code in CODES]

    def load(index):
        return pltpu.make_async_copy(
            weight.at[pl.ds(pl.multiple_of(index * per_block, per_block), per_block), :], deq.at[index], load_sem.at[index]
        )

    def start_load(index, carry):
        load(partner(me, code_at(index))).start()
        return carry

    lax.fori_loop(0, NCOL, start_load, 0)

    barrier = pltpu.get_barrier_semaphore()
    for peer in peers:
        pl.semaphore_signal(barrier, inc=1, device_id=(row, peer), device_id_type=MESH)
    for other in (1, 2, 3):
        pl.semaphore_signal(barrier, inc=1, device_id=((row + other) % 4, me), device_id_type=MESH)

    factor_top[...] = jnp.zeros(factor_top.shape, BF16)
    factor_bot[...] = jnp.zeros(factor_bot.shape, BF16)
    turned = sketch[...]
    factor_top[0:RANK, :] = turned
    factor_bot[RANK : 2 * RANK, :] = turned

    levels = [codebook[k] for k in range(LEVELS)]
    middles = []
    for k in range(LEVELS - 1):
        middle = (levels[k] + levels[k + 1]) * 0.5
        middles.append(middle + jnp.abs(middle) * 2.0**-21)

    pl.semaphore_wait(barrier, len(peers) + 3)

    def send_rows(peer, first, count, sem=None):
        rows = slice(first, first + count)
        copy = pltpu.make_async_remote_copy(
            src_ref=deq.at[peer, rows], dst_ref=quant.at[rows, pl.ds(pl.multiple_of(me * cols, 128), cols)],
            send_sem=block_sem.at[0] if sem is None else sem, recv_sem=block_sem.at[1],
            device_id=(row, peer), device_id_type=MESH,
        )
        copy.start()
        return copy

    def send_scales(peer):
        pltpu.make_async_remote_copy(
            src_ref=scale_out.at[peer], dst_ref=scales.at[me],
            send_sem=scale_sem.at[0], recv_sem=scale_sem.at[1], device_id=(row, peer), device_id_type=MESH,
        ).start()

    lane = lax.broadcasted_iota(jnp.int32, (16, 128), 1)

    def quantize_block(place, carry):
        block = partner(me, code_at(place))
        load(block).wait()

        def quantize_rows(group, inner):
            rows = pl.ds(pl.multiple_of(group * 16, 16), 16)
            shift = group // 2 * 32
            gathered = jnp.zeros((16, 128), F32)
            for tile in range(tiles):
                columns = slice(tile * 128, tile * 128 + 128)
                value = deq[block, rows, columns].astype(F32)
                size = jnp.abs(value)
                left = jnp.max(jnp.where(lane < BLOCK, size, 0.0), axis=1, keepdims=True)
                right = jnp.max(jnp.where(lane < BLOCK, 0.0, size), axis=1, keepdims=True)
                gathered = jnp.where(lane == shift + 2 * tile, left, gathered)
                gathered = jnp.where(lane == shift + 2 * tile + 1, right, gathered)
                spread = jnp.where(lane < BLOCK, left, right)
                unit_value = value * (1.0 / spread)
                level = jnp.full((16, 128), levels[0], F32)
                for k in range(LEVELS - 1):
                    level = jnp.where(unit_value > middles[k], levels[k + 1], level)
                dequant = level * spread
                deq[block, rows, columns] = dequant.astype(BF16)
                res[block, group // 3, pl.ds(pl.multiple_of(group % 3 * 16, 16), 16), columns] = (value - dequant).astype(BF16)
            held = pl.ds(pl.multiple_of(group % 2 * 16, 16), 16)
            before = scale_out[block, held, :].astype(F32)
            scale_out[block, held, :] = jnp.where(lane < shift, before, gathered).astype(BF16)
            return inner

        lax.fori_loop(0, per_block // 16, quantize_rows, 0)

        @pl.when((place % SPACING == 1) & (place // SPACING < EARLY))
        def _():
            for member in range(2):
                peer = partner(me, code_at(place // SPACING * 2 + member))
                send_rows(peer, 0, per_block)
                send_scales(peer)

        return carry

    scale_out[...] = jnp.zeros(scale_out.shape, BF16)
    lax.fori_loop(0, NCOL, quantize_block, 0)

    own = [
        pltpu.make_async_copy(deq.at[me], quant.at[:, pl.ds(pl.multiple_of(me * cols, 128), cols)], own_sem.at[0]),
        pltpu.make_async_copy(scale_out.at[me], scales.at[me], own_sem.at[1]),
    ]

    rounds, place = [], 0
    for group in ROUNDS:
        rounds.append(peers[place : place + len(group)])
        place += len(group)
    rounds = rounds[EARLY:]
    pieces = [(group, cut) for group in rounds for cut in range(CUTS)]
    state = {"sent": 0, "point": 0}

    def breathe():
        count = PACE[state["point"]]
        state["point"] += 1
        for group, cut in pieces[state["sent"] : state["sent"] + count]:
            for peer in group:
                send_rows(peer, cut * (per_block // CUTS), per_block // CUTS)
                if cut == 0:
                    send_scales(peer)
        state["sent"] += count

    def send_rest():
        rest = [(peer, cut) for group, cut in pieces[state["sent"] :] for peer in group]
        copies = []
        for place, (peer, cut) in enumerate(rest):
            if place >= WINDOW:
                copies[place - WINDOW].wait_send()
            copies.append(send_rows(peer, cut * (per_block // CUTS), per_block // CUTS, tail_sem.at[place % WINDOW]))
            if cut == 0:
                send_scales(peer)
        for copy in copies[-WINDOW:]:
            copy.wait_send()
        return len(rest) * (per_block // CUTS)

    def sample(step):
        breathe()
        def some(turn, carry):
            part = (me // 8 + turn + 1) % 4
            blocks = pl.ds(pl.multiple_of(part * 8, 8), 8)
            top = res[blocks, 0].reshape(8 * half, cols)
            bottom = res[blocks, 1].reshape(8 * half, cols)
            both = dot_nt(top, factor_top[...]) + dot_nt(bottom, factor_bot[...])
            both = both[:, 0:128] + both[:, 128:256]
            sample_out[blocks] = both.reshape(8, half, 128).astype(BF16)
            for near in range(7, -1, -1):
                peer = part * 8 + (me // 4 + near // 4) % 2 * 4 + (me + near) % 4

                @pl.when(peer != me)
                def _():
                    pltpu.make_async_remote_copy(
                        src_ref=sample_out.at[peer], dst_ref=reduce_in.at[step, me],
                        send_sem=reduce_sem.at[step, 0], recv_sem=reduce_sem.at[step, 1],
                        device_id=(row, peer), device_id_type=MESH,
                    ).start()

            return carry

        lax.fori_loop(0, NCOL // 8, some, 0)
        reduce_in[step, pl.ds(me, 1)] = sample_out[pl.ds(me, 1)]
        breathe()
        drain(reduce_in.at[step, 0 : NCOL - 1], reduce_sem.at[step, 1])
        mine = jnp.sum(reduce_in[step].astype(F32), axis=0)
        gather_in[step, pl.ds(me, 1)] = mine.astype(BF16)[None]
        for peer in peers:
            pltpu.make_async_remote_copy(
                src_ref=gather_in.at[step, me], dst_ref=gather_in.at[step, me],
                send_sem=gather_sem.at[step, 0], recv_sem=gather_sem.at[step, 1], device_id=(row, peer), device_id_type=MESH,
            ).start()
        breathe()
        drain(reduce_in.at[step, 0 : NCOL - 1], reduce_sem.at[step, 0])
        drain(gather_in.at[step, 0 : NCOL - 1], gather_sem.at[step, 1])

    def begin_gram(step):
        packed = gather_in[step].reshape(NCOL * half, 128)
        sample_t[...] = packed.astype(F32).T.astype(BF16)
        gram = dot(sample_t[...], packed)
        gram = gram[0:RANK] + pltpu.roll(gram[RANK : 2 * RANK], RANK, 1)
        gram_out[step] = gram
        gram_in[step, pl.ds(row, 1)] = gram[None]
        for other in (1, 2, 3):
            pltpu.make_async_remote_copy(
                src_ref=gram_out.at[step], dst_ref=gram_in.at[step, row],
                send_sem=gram_sem.at[step, 0], recv_sem=gram_sem.at[step, 1],
                device_id=((row + other) % 4, me), device_id_type=MESH,
            ).start()

    def end_gram(step):
        drain(gram_in.at[step, 0:3], gram_sem.at[step, 1])
        drain(gram_in.at[step, 0:3], gram_sem.at[step, 0])
        gram = (gram_in[step, 0] + gram_in[step, 1]) + (gram_in[step, 2] + gram_in[step, 3])
        lanes = lax.broadcasted_iota(jnp.int32, (RANK, 128), 1)
        subs = lax.broadcasted_iota(jnp.int32, (RANK, 128), 0)
        work[...] = jnp.where(lanes < RANK, gram, jnp.where(lanes - RANK == subs, 1.0, 0.0))

    def eliminate(first, last):
        lanes = lax.broadcasted_iota(jnp.int32, (RANK, 128), 1)
        subs = lax.broadcasted_iota(jnp.int32, (RANK, 1), 0)

        def pivot(k, carry):
            held = work[...]
            line = work[pl.ds(k, 1), :]
            column = jnp.sum(jnp.where(lanes == k, held, 0.0), axis=1, keepdims=True)
            top = jnp.sum(jnp.where(lanes[0:1] == k, line, 0.0), axis=1, keepdims=True)
            scaled = jnp.where(subs > k, column, 0.0) * (1.0 / top)
            work[...] = held - scaled * line
            return carry

        lax.fori_loop(first, last, pivot, 0)

    def inverse_factor():
        lanes = lax.broadcasted_iota(jnp.int32, (RANK, 128), 1)
        subs = lax.broadcasted_iota(jnp.int32, (RANK, 128), 0)
        held = work[...]
        pivots = jnp.sum(jnp.where(lanes == subs, held, 0.0), axis=1, keepdims=True)
        return jnp.where(lanes < RANK, 0.0, held * (1.0 / jnp.sqrt(pivots)))

    def project_all(step):
        breathe()
        project[...] = jnp.zeros(project.shape, F32)

        def some(part, carry):
            blocks = pl.ds(pl.multiple_of(part * 16, 16), 16)
            depth = pl.ds(pl.multiple_of(part * 16 * half, 128), 16 * half)
            top = res[blocks, 0].reshape(16 * half, cols)
            bottom = res[blocks, 1].reshape(16 * half, cols)
            project[...] += dot(sample_t[0:RANK, depth], top) + dot(sample_t[RANK : 2 * RANK, depth], bottom)
            return carry

        lax.fori_loop(0, NCOL // 16, some, 0)

    def reduce_project(step):
        part = RANK // 2
        mine = pl.ds(pl.multiple_of(core * part, part), part)
        other = pl.ds(pl.multiple_of((1 - core) * part, part), part)
        one = pltpu.make_async_remote_copy(
            src_ref=project.at[other, :], dst_ref=half_in.at[step],
            send_sem=half_sem.at[step, 0], recv_sem=half_sem.at[step, 1], device_id=(mate, me), device_id_type=MESH,
        )
        one.start()
        breathe()
        end_gram(step)
        one.wait()
        sent, met = (pair_out, pair_in.at[step]) if step < POWER else (last_out, last_in)
        sent[...] = (project[mine, :] + half_in[step]).astype(sent.dtype)
        two = pltpu.make_async_remote_copy(
            src_ref=sent, dst_ref=met,
            send_sem=pair_sem.at[step, 0], recv_sem=pair_sem.at[step, 1], device_id=(across, me), device_id_type=MESH,
        )
        two.start()
        breathe()
        eliminate(0, RANK // 2)
        two.wait()
        total[step, mine, :] = sent[...].astype(F32) + met[...].astype(F32)
        three = pltpu.make_async_remote_copy(
            src_ref=total.at[step, mine, :], dst_ref=total.at[step, mine, :],
            send_sem=total_sem.at[step, 0], recv_sem=total_sem.at[step, 1], device_id=(mate, me), device_id_type=MESH,
        )
        three.start()
        breathe()
        eliminate(RANK // 2, RANK)
        three.wait()

    root = math.sqrt(ROWS)
    for step in range(POWER + 1):
        sample(step)
        if step == 0:
            for copy in own:
                copy.start()
        begin_gram(step)
        project_all(step)
        reduce_project(step)
        inverse = inverse_factor()
        factor = dot(pltpu.roll(inverse, RANK, 1)[:, 0:RANK], total[step], HIGH)
        if step < POWER:
            upper = factor.astype(BF16)
            lower = (factor - upper.astype(F32)).astype(BF16)
            factor_top[0:RANK, :] = upper
            factor_top[2 * RANK : 3 * RANK, :] = lower
            factor_bot[RANK : 2 * RANK, :] = upper
            factor_bot[3 * RANK : 4 * RANK, :] = lower
        else:
            lora_b[...] = factor * (1.0 / root)
            packed = gather_in[step].reshape(NCOL * half, 128).astype(F32)
            right = inverse * root
            left = pltpu.roll(right, RANK, 1)
            lora_a[:, 0] = dot_nt(packed, left, HIGH).reshape(NCOL, half, RANK)
            lora_a[:, 1] = dot_nt(packed, right, HIGH).reshape(NCOL, half, RANK)
        drain(gather_in.at[step, 0 : NCOL - 1], gather_sem.at[step, 0])
    apart = send_rest()

    for copy in own:
        copy.wait()
    drain(scale_out.at[0 : NCOL - 1], scale_sem.at[0])
    drain(scales.at[0 : NCOL - 1], scale_sem.at[1])
    whole, over = divmod((NCOL - 1) * per_block - apart, per_block)
    drain(deq.at[0:whole], block_sem.at[0])
    if over:
        drain(deq.at[0, 0:over], block_sem.at[0])
    drain(quant.at[:, pl.ds(0, (NCOL - 1) * cols)], block_sem.at[1])


def finish(quant_in, pieces, basis, lora_b_in, quant, scales, lora_a, lora_b, held, sems):
    strips = [slice(16 * k, 16 * k + 16) for k in range(quant.shape[0] // 16)]
    loads = [pltpu.make_async_copy(quant_in.at[strip], held.at[strip], sems.at[0, k]) for k, strip in enumerate(strips)]
    stores = [pltpu.make_async_copy(held.at[strip], quant.at[strip], sems.at[1, k]) for k, strip in enumerate(strips)]
    for copy in loads:
        copy.start()
    lora_b[...] = lora_b_in[...]
    lora_a[...] = basis[...].T
    width = scales.shape[1] // NCOL
    lane = lax.broadcasted_iota(jnp.int32, (32, 128), 1)
    for group in range(scales.shape[0] // 32):
        for load, store in zip(loads[2 * group : 2 * group + 2], stores[2 * group : 2 * group + 2]):
            load.wait()
            store.start()
        rows = slice(32 * group, 32 * group + 32)
        found = [jnp.zeros((32, 128), F32) for _ in range(scales.shape[1] // 128 + 1)]
        for source in range(NCOL):
            start = source * width
            tile, first = start // 128, start % 128
            turned = pltpu.roll(pieces[source].astype(F32), (first - 32 * group) % 128, 1)
            found[tile] = jnp.where((lane >= first) & (lane < first + width), turned, found[tile])
            if first + width > 128:
                found[tile + 1] = jnp.where(lane < first + width - 128, turned, found[tile + 1])
        for tile, part in enumerate(found):
            left = min(128, scales.shape[1] - 128 * tile)
            if left > 0:
                scales[rows, 128 * tile : 128 * tile + left] = part[:, :left]
    for copy in stores:
        copy.wait()


def body(weight, sketch, codebook):
    rows, cols = weight.shape
    per_block = rows // NCOL
    half = per_block // 2
    steps = POWER + 1
    anywhere = pl.BlockSpec(memory_space=pl.ANY)
    local = pl.BlockSpec(memory_space=pltpu.VMEM)
    dma = pltpu.SemaphoreType.DMA
    quant, scales, lora_a, lora_b = pl.pallas_call(
        kernel,
        name="loftq",
        out_shape=(
            jax.ShapeDtypeStruct((per_block, NCOL * cols), BF16),
            jax.ShapeDtypeStruct((NCOL, 32, 128), BF16),
            jax.ShapeDtypeStruct((NCOL, 2, half, RANK), F32),
            jax.ShapeDtypeStruct((RANK, cols), F32),
        ),
        in_specs=[anywhere, local, pl.BlockSpec(memory_space=pltpu.SMEM)],
        out_specs=(anywhere, anywhere, local, local),
        scratch_shapes=[
            pltpu.VMEM((NCOL, per_block, cols), BF16),
            pltpu.VMEM((NCOL, 2, half, cols), BF16),
            pltpu.VMEM((NCOL, 32, 128), BF16),
            pltpu.VMEM((4 * RANK, cols), BF16),
            pltpu.VMEM((4 * RANK, cols), BF16),
            pltpu.VMEM((NCOL, half, 128), BF16),
            pltpu.VMEM((steps, NCOL, half, 128), BF16),
            pltpu.VMEM((steps, NCOL, half, 128), BF16),
            pltpu.VMEM((128, NCOL * half), BF16),
            pltpu.VMEM((RANK, cols), F32),
            pltpu.VMEM((steps, RANK // 2, cols), F32),
            pltpu.VMEM((RANK // 2, cols), BF16),
            pltpu.VMEM((POWER, RANK // 2, cols), BF16),
            pltpu.VMEM((RANK // 2, cols), F32),
            pltpu.VMEM((RANK // 2, cols), F32),
            pltpu.VMEM((steps, RANK, cols), F32),
            pltpu.VMEM((steps, 4, RANK, 128), F32),
            pltpu.VMEM((steps, RANK, 128), F32),
            pltpu.VMEM((RANK, 128), F32),
            dma((NCOL,)),
            dma((2,)),
            dma((2,)),
            dma((2,)),
            dma((steps, 2)),
            dma((steps, 2)),
            dma((steps, 2)),
            dma((steps, 2)),
            dma((steps, 2)),
            dma((steps, 2)),
            dma((WINDOW,)),
        ],
        compiler_params=pltpu.CompilerParams(
            collective_id=0, has_side_effects=True, vmem_limit_bytes=56 * 1024 * 1024
        ),
    )(weight, sketch.T, codebook.astype(F32))
    quant, scales, lora_a, lora_b = pl.pallas_call(
        finish,
        name="finish",
        out_shape=(
            jax.ShapeDtypeStruct((per_block, NCOL * cols), BF16),
            jax.ShapeDtypeStruct((per_block, NCOL * cols // BLOCK), F32),
            jax.ShapeDtypeStruct((RANK, rows), F32),
            jax.ShapeDtypeStruct((RANK, cols), F32),
        ),
        in_specs=[anywhere, local, local, local],
        out_specs=(anywhere, local, local, local),
        scratch_shapes=[pltpu.VMEM((per_block, NCOL * cols), BF16), dma((2, per_block // 16))],
        compiler_params=pltpu.CompilerParams(vmem_limit_bytes=58 * 1024 * 1024),
    )(quant, scales, lora_a.reshape(rows, RANK), lora_b)
    return quant, scales, lora_a.T, lora_b


def solution(mesh):
    in_specs = (P("row", "col"), P("col", None), P())
    out_specs = (P(("row", "col"), None), P(("row", "col"), None), P("row", None), P(None, "col"))
    return jax.shard_map(body, mesh=mesh, in_specs=in_specs, out_specs=out_specs, check_vma=False)
```

```python
import functools
import math

import jax
import jax.numpy as jnp
from jax import lax
from jax.experimental import pallas as pl
from jax.experimental.pallas import tpu as pltpu
from jax.sharding import PartitionSpec as P

ROWS = 12288
BLOCK = 64
POWER = 2
LEVELS = 16
RANK = 64
NCOL = 32
HIGH = lax.Precision.HIGHEST
MESH = pl.DeviceIdType.MESH
F32 = jnp.float32
BF16 = jnp.bfloat16

ROUNDS = (
    ((1, 1, 0), (3, 3, 1)),
    ((1, 1, 1), (3, 3, 0)),
    ((1, 3, 0), (3, 1, 1)),
    ((1, 3, 1), (3, 1, 0)),
    ((2, 0, 0), (0, 2, 1)),
    ((2, 0, 1), (0, 2, 0)),
    ((2, 1, 0), (0, 3, 1)),
    ((2, 1, 1), (0, 3, 0)),
    ((2, 3, 0), (0, 1, 1)),
    ((2, 3, 1), (0, 1, 0)),
    ((1, 2, 0), (3, 0, 1)),
    ((1, 2, 1), (3, 0, 0)),
    ((3, 2, 0), (1, 0, 1)),
    ((3, 2, 1), (1, 0, 0)),
    ((2, 2, 1),),
    ((2, 2, 0), (0, 0, 1)),
)
CODES = tuple(dx + 4 * dy + 16 * dz for group in ROUNDS for dx, dy, dz in group)
EARLY = 6
SPACING = 5
CUTS = 6
PACE = (0, 0, 1, 2, 0, 2, 4) * 3
WINDOW = 12


def partner(me, code):
    x, y, z = (me // 4) % 4, me % 4, me // 16
    dx, dy, dz = code % 4, (code // 4) % 4, code // 16
    return (z + dz) % 2 * 16 + (x + dx) % 4 * 4 + (y + dy) % 4


def code_at(index):
    code = 0
    for place, value in enumerate(CODES):
        code = jnp.where(index == place, value, code)
    return code


def dot(a, b, precision=None):
    return lax.dot_general(a, b, (((1,), (0,)), ((), ())), precision=precision, preferred_element_type=F32)


def dot_nt(a, b, precision=None):
    return lax.dot_general(a, b, (((1,), (1,)), ((), ())), precision=precision, preferred_element_type=F32)


def drain(ref, sem):
    pltpu.make_async_copy(ref, ref, sem).wait()


def kernel(
    weight, sketch, codebook,
    quant, scales, lora_a, lora_b,
    deq, res, scale_out, scale_in, basis, factor_top, factor_bot, sample_out, reduce_in, gather_in, sample_t,
    project, half_in, pair_out, pair_in, last_out, last_in, total, gram_in, gram_out, work,
    load_sem, block_sem, scale_sem, own_sem, reduce_sem, gather_sem, half_sem, pair_sem, total_sem, gram_sem, tail_sem,
):
    cols = deq.shape[2]
    tiles = cols // 128
    per_block = deq.shape[1]
    half = per_block // 2
    row, me = lax.axis_index("row"), lax.axis_index("col")
    core = row % 2
    mate = row + 1 - 2 * core
    across = (row + 2) % 4
    peers = [partner(me, code) for code in CODES]

    def load(index):
        return pltpu.make_async_copy(
            weight.at[pl.ds(pl.multiple_of(index * per_block, per_block), per_block), :], deq.at[index], load_sem.at[index]
        )

    def start_load(index, carry):
        load(partner(me, code_at(index))).start()
        return carry

    lax.fori_loop(0, NCOL, start_load, 0)

    barrier = pltpu.get_barrier_semaphore()
    for peer in peers:
        pl.semaphore_signal(barrier, inc=1, device_id=(row, peer), device_id_type=MESH)
    for other in (1, 2, 3):
        pl.semaphore_signal(barrier, inc=1, device_id=((row + other) % 4, me), device_id_type=MESH)

    factor_top[...] = jnp.zeros(factor_top.shape, BF16)
    factor_bot[...] = jnp.zeros(factor_bot.shape, BF16)
    turned = sketch[...]
    factor_top[0:RANK, :] = turned
    factor_bot[RANK : 2 * RANK, :] = turned

    levels = [codebook[k] for k in range(LEVELS)]
    middles = []
    for k in range(LEVELS - 1):
        middle = (levels[k] + levels[k + 1]) * 0.5
        middles.append(middle + jnp.abs(middle) * 2.0**-21)

    pl.semaphore_wait(barrier, len(peers) + 3)

    def send_rows(peer, first, count, sem=None):
        rows = slice(first, first + count)
        copy = pltpu.make_async_remote_copy(
            src_ref=deq.at[peer, rows], dst_ref=quant.at[rows, pl.ds(pl.multiple_of(me * cols, 128), cols)],
            send_sem=block_sem.at[0] if sem is None else sem, recv_sem=block_sem.at[1],
            device_id=(row, peer), device_id_type=MESH,
        )
        copy.start()
        return copy

    def send_scales(peer):
        pltpu.make_async_remote_copy(
            src_ref=scale_out.at[peer], dst_ref=scale_in.at[me],
            send_sem=scale_sem.at[0], recv_sem=scale_sem.at[1], device_id=(row, peer), device_id_type=MESH,
        ).start()

    lane = lax.broadcasted_iota(jnp.int32, (16, 128), 1)

    def quantize_block(place, carry):
        block = partner(me, code_at(place))
        load(block).wait()

        def quantize_rows(group, inner):
            rows = pl.ds(pl.multiple_of(group * 16, 16), 16)
            shift = group // 2 * 32
            gathered = jnp.zeros((16, 128), F32)
            for tile in range(tiles):
                columns = slice(tile * 128, tile * 128 + 128)
                value = deq[block, rows, columns].astype(F32)
                size = jnp.abs(value)
                left = jnp.max(jnp.where(lane < BLOCK, size, 0.0), axis=1, keepdims=True)
                right = jnp.max(jnp.where(lane < BLOCK, 0.0, size), axis=1, keepdims=True)
                gathered = jnp.where(lane == shift + 2 * tile, left, gathered)
                gathered = jnp.where(lane == shift + 2 * tile + 1, right, gathered)
                spread = jnp.where(lane < BLOCK, left, right)
                unit_value = value * (1.0 / spread)
                level = jnp.full((16, 128), levels[0], F32)
                for k in range(LEVELS - 1):
                    level = jnp.where(unit_value > middles[k], levels[k + 1], level)
                dequant = level * spread
                deq[block, rows, columns] = dequant.astype(BF16)
                res[block, group // 3, pl.ds(pl.multiple_of(group % 3 * 16, 16), 16), columns] = (value - dequant).astype(BF16)
            held = pl.ds(pl.multiple_of(group % 2 * 16, 16), 16)
            before = scale_out[block, held, :].astype(F32)
            scale_out[block, held, :] = jnp.where(lane < shift, before, gathered).astype(BF16)
            return inner

        lax.fori_loop(0, per_block // 16, quantize_rows, 0)

        @pl.when((place % SPACING == 1) & (place // SPACING < EARLY))
        def _():
            for member in range(2):
                peer = partner(me, code_at(place // SPACING * 2 + member))
                send_rows(peer, 0, per_block)
                send_scales(peer)

        return carry

    scale_out[...] = jnp.zeros(scale_out.shape, BF16)
    lax.fori_loop(0, NCOL, quantize_block, 0)

    own = [
        pltpu.make_async_copy(deq.at[me], quant.at[:, pl.ds(pl.multiple_of(me * cols, 128), cols)], own_sem.at[0]),
        pltpu.make_async_copy(scale_out.at[me], scale_in.at[me], own_sem.at[1]),
    ]

    rounds, place = [], 0
    for group in ROUNDS:
        rounds.append(peers[place : place + len(group)])
        place += len(group)
    rounds = rounds[EARLY:]
    pieces = [(group, cut) for group in rounds for cut in range(CUTS)]
    state = {"sent": 0, "point": 0}

    def breathe():
        count = PACE[state["point"]]
        state["point"] += 1
        for group, cut in pieces[state["sent"] : state["sent"] + count]:
            for peer in group:
                send_rows(peer, cut * (per_block // CUTS), per_block // CUTS)
                if cut == 0:
                    send_scales(peer)
        state["sent"] += count

    rest = []

    def begin_rest():
        for group, cut in pieces[state["sent"] :]:
            rest.extend((peer, cut) for peer in group)
        for peer, cut in rest:
            if cut == 0:
                send_scales(peer)
        tail.extend(send_tail(place) for place in range(min(WINDOW, len(rest))))

    tail = []

    def send_tail(place):
        peer, cut = rest[place]
        return send_rows(peer, cut * (per_block // CUTS), per_block // CUTS, tail_sem.at[place % WINDOW])

    def end_rest():
        for place in range(WINDOW, len(rest)):
            tail[place - WINDOW].wait_send()
            tail.append(send_tail(place))

    def place_scales():
        width = scales.shape[1] // NCOL
        lanes = lax.broadcasted_iota(jnp.int32, (32, 128), 1)
        for group in range(per_block // 32):
            rows = slice(32 * group, 32 * group + 32)
            found = [jnp.zeros((32, 128), F32) for _ in range(scales.shape[1] // 128 + 1)]
            for source in range(NCOL):
                start = source * width
                tile, first = start // 128, start % 128
                turned = pltpu.roll(scale_in[source].astype(F32), (first - 32 * group) % 128, 1)
                found[tile] = jnp.where((lanes >= first) & (lanes < first + width), turned, found[tile])
                if first + width > 128:
                    found[tile + 1] = jnp.where(lanes < first + width - 128, turned, found[tile + 1])
            for tile, part in enumerate(found):
                left = min(128, scales.shape[1] - 128 * tile)
                if left > 0:
                    scales[rows, 128 * tile : 128 * tile + left] = part[:, :left]

    def sample(step):
        breathe()
        def some(turn, carry):
            part = (me // 8 + turn + 1) % 4
            blocks = pl.ds(pl.multiple_of(part * 8, 8), 8)
            top = res[blocks, 0].reshape(8 * half, cols)
            bottom = res[blocks, 1].reshape(8 * half, cols)
            both = dot_nt(top, factor_top[...]) + dot_nt(bottom, factor_bot[...])
            both = both[:, 0:128] + both[:, 128:256]
            sample_out[blocks] = both.reshape(8, half, 128).astype(BF16)
            for near in range(7, -1, -1):
                peer = part * 8 + (me // 4 + near // 4) % 2 * 4 + (me + near) % 4

                @pl.when(peer != me)
                def _():
                    pltpu.make_async_remote_copy(
                        src_ref=sample_out.at[peer], dst_ref=reduce_in.at[step, me],
                        send_sem=reduce_sem.at[step, 0], recv_sem=reduce_sem.at[step, 1],
                        device_id=(row, peer), device_id_type=MESH,
                    ).start()

            return carry

        lax.fori_loop(0, NCOL // 8, some, 0)
        reduce_in[step, pl.ds(me, 1)] = sample_out[pl.ds(me, 1)]
        breathe()
        drain(reduce_in.at[step, 0 : NCOL - 1], reduce_sem.at[step, 1])
        mine = jnp.sum(reduce_in[step].astype(F32), axis=0)
        gather_in[step, pl.ds(me, 1)] = mine.astype(BF16)[None]
        for peer in peers:
            pltpu.make_async_remote_copy(
                src_ref=gather_in.at[step, me], dst_ref=gather_in.at[step, me],
                send_sem=gather_sem.at[step, 0], recv_sem=gather_sem.at[step, 1], device_id=(row, peer), device_id_type=MESH,
            ).start()
        breathe()
        drain(reduce_in.at[step, 0 : NCOL - 1], reduce_sem.at[step, 0])
        drain(gather_in.at[step, 0 : NCOL - 1], gather_sem.at[step, 1])

    def begin_gram(step):
        packed = gather_in[step].reshape(NCOL * half, 128)
        sample_t[...] = packed.astype(F32).T.astype(BF16)
        gram = dot(sample_t[...], packed)
        gram = gram[0:RANK] + pltpu.roll(gram[RANK : 2 * RANK], RANK, 1)
        gram_out[step] = gram
        gram_in[step, pl.ds(row, 1)] = gram[None]
        for other in (1, 2, 3):
            pltpu.make_async_remote_copy(
                src_ref=gram_out.at[step], dst_ref=gram_in.at[step, row],
                send_sem=gram_sem.at[step, 0], recv_sem=gram_sem.at[step, 1],
                device_id=((row + other) % 4, me), device_id_type=MESH,
            ).start()

    def end_gram(step):
        drain(gram_in.at[step, 0:3], gram_sem.at[step, 1])
        drain(gram_in.at[step, 0:3], gram_sem.at[step, 0])
        gram = (gram_in[step, 0] + gram_in[step, 1]) + (gram_in[step, 2] + gram_in[step, 3])
        lanes = lax.broadcasted_iota(jnp.int32, (RANK, 128), 1)
        subs = lax.broadcasted_iota(jnp.int32, (RANK, 128), 0)
        work[...] = jnp.where(lanes < RANK, gram, jnp.where(lanes - RANK == subs, 1.0, 0.0))

    def eliminate(first, last):
        lanes = lax.broadcasted_iota(jnp.int32, (RANK, 128), 1)
        subs = lax.broadcasted_iota(jnp.int32, (RANK, 1), 0)

        def pivot(k, carry):
            held = work[...]
            line = work[pl.ds(k, 1), :]
            column = jnp.sum(jnp.where(lanes == k, held, 0.0), axis=1, keepdims=True)
            top = jnp.sum(jnp.where(lanes[0:1] == k, line, 0.0), axis=1, keepdims=True)
            scaled = jnp.where(subs > k, column, 0.0) * (1.0 / top)
            work[...] = held - scaled * line
            return carry

        lax.fori_loop(first, last, pivot, 0)

    def inverse_factor():
        lanes = lax.broadcasted_iota(jnp.int32, (RANK, 128), 1)
        subs = lax.broadcasted_iota(jnp.int32, (RANK, 128), 0)
        held = work[...]
        pivots = jnp.sum(jnp.where(lanes == subs, held, 0.0), axis=1, keepdims=True)
        return jnp.where(lanes < RANK, 0.0, held * (1.0 / jnp.sqrt(pivots)))

    def project_all(step):
        breathe()
        project[...] = jnp.zeros(project.shape, F32)

        def some(part, carry):
            blocks = pl.ds(pl.multiple_of(part * 16, 16), 16)
            depth = pl.ds(pl.multiple_of(part * 16 * half, 128), 16 * half)
            top = res[blocks, 0].reshape(16 * half, cols)
            bottom = res[blocks, 1].reshape(16 * half, cols)
            project[...] += dot(sample_t[0:RANK, depth], top) + dot(sample_t[RANK : 2 * RANK, depth], bottom)
            return carry

        lax.fori_loop(0, NCOL // 16, some, 0)

    def reduce_project(step):
        part = RANK // 2
        mine = pl.ds(pl.multiple_of(core * part, part), part)
        other = pl.ds(pl.multiple_of((1 - core) * part, part), part)
        one = pltpu.make_async_remote_copy(
            src_ref=project.at[other, :], dst_ref=half_in.at[step],
            send_sem=half_sem.at[step, 0], recv_sem=half_sem.at[step, 1], device_id=(mate, me), device_id_type=MESH,
        )
        one.start()
        breathe()
        end_gram(step)
        one.wait()
        sent, met = (pair_out, pair_in.at[step]) if step < POWER else (last_out, last_in)
        sent[...] = (project[mine, :] + half_in[step]).astype(sent.dtype)
        two = pltpu.make_async_remote_copy(
            src_ref=sent, dst_ref=met,
            send_sem=pair_sem.at[step, 0], recv_sem=pair_sem.at[step, 1], device_id=(across, me), device_id_type=MESH,
        )
        two.start()
        breathe()
        eliminate(0, RANK // 2)
        two.wait()
        total[step, mine, :] = sent[...].astype(F32) + met[...].astype(F32)
        three = pltpu.make_async_remote_copy(
            src_ref=total.at[step, mine, :], dst_ref=total.at[step, mine, :],
            send_sem=total_sem.at[step, 0], recv_sem=total_sem.at[step, 1], device_id=(mate, me), device_id_type=MESH,
        )
        three.start()
        breathe()
        eliminate(RANK // 2, RANK)
        three.wait()

    root = math.sqrt(ROWS)
    for step in range(POWER + 1):
        sample(step)
        if step == 0:
            for copy in own:
                copy.start()
        begin_gram(step)
        project_all(step)
        reduce_project(step)
        inverse = inverse_factor()
        factor = dot(pltpu.roll(inverse, RANK, 1)[:, 0:RANK], total[step], HIGH)
        if step < POWER:
            upper = factor.astype(BF16)
            lower = (factor - upper.astype(F32)).astype(BF16)
            factor_top[0:RANK, :] = upper
            factor_top[2 * RANK : 3 * RANK, :] = lower
            factor_bot[RANK : 2 * RANK, :] = upper
            factor_bot[3 * RANK : 4 * RANK, :] = lower
        else:
            begin_rest()
            lora_b[...] = factor * (1.0 / root)
            packed = gather_in[step].reshape(NCOL * half, 128).astype(F32)
            right = inverse * root
            left = pltpu.roll(right, RANK, 1)
            basis[:, 0] = dot_nt(packed, left, HIGH).reshape(NCOL, half, RANK)
            basis[:, 1] = dot_nt(packed, right, HIGH).reshape(NCOL, half, RANK)
            lora_a[...] = basis[...].reshape(lora_a.shape[1], RANK).T
        drain(gather_in.at[step, 0 : NCOL - 1], gather_sem.at[step, 0])
    end_rest()
    for copy in own:
        copy.wait()
    drain(scale_out.at[0 : NCOL - 1], scale_sem.at[0])
    drain(scale_in.at[0 : NCOL - 1], scale_sem.at[1])
    place_scales()
    for copy in tail[-WINDOW:]:
        copy.wait_send()
    apart = len(rest) * (per_block // CUTS)
    whole, over = divmod((NCOL - 1) * per_block - apart, per_block)
    drain(deq.at[0:whole], block_sem.at[0])
    if over:
        drain(deq.at[0, 0:over], block_sem.at[0])
    drain(quant.at[:, pl.ds(0, (NCOL - 1) * cols)], block_sem.at[1])


def finish(*refs):
    count = len(refs) // 3
    sources, targets, held, (load_sem, store_sem) = refs[:count], refs[count : 2 * count], refs[2 * count : 3 * count], refs[3 * count :]
    strips = [(0, slice(16 * k, 16 * k + 16)) for k in range(sources[0].shape[0] // 16)]
    strips += [(k, slice(0, sources[k].shape[0])) for k in range(1, count)]
    loads, stores = [], []
    for place, (k, rows) in enumerate(strips):
        loads.append(pltpu.make_async_copy(sources[k].at[rows], held[k].at[rows], load_sem.at[place]))
        stores.append(pltpu.make_async_copy(held[k].at[rows], targets[k].at[rows], store_sem.at[place]))
    for load in loads:
        load.start()
    for load, store in zip(loads, stores):
        load.wait()
        store.start()
    for store in stores:
        store.wait()


def body(weight, sketch, codebook):
    rows, cols = weight.shape
    per_block = rows // NCOL
    half = per_block // 2
    steps = POWER + 1
    anywhere = pl.BlockSpec(memory_space=pl.ANY)
    local = pl.BlockSpec(memory_space=pltpu.VMEM)
    dma = pltpu.SemaphoreType.DMA
    quant, scales, lora_a, lora_b = pl.pallas_call(
        kernel,
        name="loftq",
        out_shape=(
            jax.ShapeDtypeStruct((per_block, NCOL * cols), BF16),
            jax.ShapeDtypeStruct((per_block, NCOL * cols // BLOCK), F32),
            jax.ShapeDtypeStruct((RANK, rows), F32),
            jax.ShapeDtypeStruct((RANK, cols), F32),
        ),
        in_specs=[anywhere, local, pl.BlockSpec(memory_space=pltpu.SMEM)],
        out_specs=(anywhere, local, local, local),
        scratch_shapes=[
            pltpu.VMEM((NCOL, per_block, cols), BF16),
            pltpu.VMEM((NCOL, 2, half, cols), BF16),
            pltpu.VMEM((NCOL, 32, 128), BF16),
            pltpu.VMEM((NCOL, 32, 128), BF16),
            pltpu.VMEM((NCOL, 2, half, RANK), F32),
            pltpu.VMEM((4 * RANK, cols), BF16),
            pltpu.VMEM((4 * RANK, cols), BF16),
            pltpu.VMEM((NCOL, half, 128), BF16),
            pltpu.VMEM((steps, NCOL, half, 128), BF16),
            pltpu.VMEM((steps, NCOL, half, 128), BF16),
            pltpu.VMEM((128, NCOL * half), BF16),
            pltpu.VMEM((RANK, cols), F32),
            pltpu.VMEM((steps, RANK // 2, cols), F32),
            pltpu.VMEM((RANK // 2, cols), BF16),
            pltpu.VMEM((POWER, RANK // 2, cols), BF16),
            pltpu.VMEM((RANK // 2, cols), F32),
            pltpu.VMEM((RANK // 2, cols), F32),
            pltpu.VMEM((steps, RANK, cols), F32),
            pltpu.VMEM((steps, 4, RANK, 128), F32),
            pltpu.VMEM((steps, RANK, 128), F32),
            pltpu.VMEM((RANK, 128), F32),
            dma((NCOL,)),
            dma((2,)),
            dma((2,)),
            dma((2,)),
            dma((steps, 2)),
            dma((steps, 2)),
            dma((steps, 2)),
            dma((steps, 2)),
            dma((steps, 2)),
            dma((steps, 2)),
            dma((WINDOW,)),
        ],
        compiler_params=pltpu.CompilerParams(
            collective_id=0, has_side_effects=True, vmem_limit_bytes=56 * 1024 * 1024
        ),
    )(weight, sketch.T, codebook.astype(F32))
    results = [quant, scales, lora_a, lora_b]
    quant, scales, lora_a, lora_b = pl.pallas_call(
        finish,
        name="finish",
        out_shape=tuple(jax.ShapeDtypeStruct(result.shape, result.dtype) for result in results),
        in_specs=[anywhere] * 4,
        out_specs=(anywhere,) * 4,
        scratch_shapes=[pltpu.VMEM(result.shape, result.dtype) for result in results]
        + [dma((per_block // 16 + 3,)), dma((per_block // 16 + 3,))],
        compiler_params=pltpu.CompilerParams(vmem_limit_bytes=58 * 1024 * 1024),
    )(*results)
    return quant, scales, lora_a.T, lora_b


def solution(mesh):
    in_specs = (P("row", "col"), P("col", None), P())
    out_specs = (P(("row", "col"), None), P(("row", "col"), None), P("row", None), P(None, "col"))
    return jax.shard_map(body, mesh=mesh, in_specs=in_specs, out_specs=out_specs, check_vma=False)
```

```python
import functools
import math

import jax
import jax.numpy as jnp
from jax import lax
from jax.experimental import pallas as pl
from jax.experimental.pallas import tpu as pltpu
from jax.sharding import PartitionSpec as P

ROWS = 12288
BLOCK = 64
POWER = 2
LEVELS = 16
RANK = 64
NCOL = 32
HIGH = lax.Precision.HIGHEST
MESH = pl.DeviceIdType.MESH
F32 = jnp.float32
BF16 = jnp.bfloat16

ROUNDS = (
    ((1, 1, 0), (3, 3, 1)),
    ((1, 1, 1), (3, 3, 0)),
    ((1, 3, 0), (3, 1, 1)),
    ((1, 3, 1), (3, 1, 0)),
    ((2, 0, 0), (0, 2, 1)),
    ((2, 0, 1), (0, 2, 0)),
    ((2, 1, 0), (0, 3, 1)),
    ((2, 1, 1), (0, 3, 0)),
    ((2, 3, 0), (0, 1, 1)),
    ((2, 3, 1), (0, 1, 0)),
    ((1, 2, 0), (3, 0, 1)),
    ((1, 2, 1), (3, 0, 0)),
    ((3, 2, 0), (1, 0, 1)),
    ((3, 2, 1), (1, 0, 0)),
    ((2, 2, 1),),
    ((2, 2, 0), (0, 0, 1)),
)
CODES = tuple(dx + 4 * dy + 16 * dz for group in ROUNDS for dx, dy, dz in group)
EARLY = 7
SPACING = 4
CUTS = 6
PACE = (0, 0, 1, 2, 0, 2, 4) * 3
WINDOW = 12


def partner(me, code):
    x, y, z = (me // 4) % 4, me % 4, me // 16
    dx, dy, dz = code % 4, (code // 4) % 4, code // 16
    return (z + dz) % 2 * 16 + (x + dx) % 4 * 4 + (y + dy) % 4


def code_at(index):
    code = 0
    for place, value in enumerate(CODES):
        code = jnp.where(index == place, value, code)
    return code


def dot(a, b, precision=None):
    return lax.dot_general(a, b, (((1,), (0,)), ((), ())), precision=precision, preferred_element_type=F32)


def dot_nt(a, b, precision=None):
    return lax.dot_general(a, b, (((1,), (1,)), ((), ())), precision=precision, preferred_element_type=F32)


def drain(ref, sem):
    pltpu.make_async_copy(ref, ref, sem).wait()


def kernel(
    weight, sketch, codebook,
    quant, scales, lora_a, lora_b,
    deq, res, scale_out, scale_in, basis, factor_top, factor_bot, sample_out, reduce_in, gather_in, sample_t,
    project, half_in, pair_out, pair_in, last_out, last_in, total, gram_in, gram_out, work,
    load_sem, block_sem, scale_sem, own_sem, reduce_sem, gather_sem, half_sem, pair_sem, total_sem, gram_sem, tail_sem,
):
    cols = deq.shape[2]
    tiles = cols // 128
    per_block = deq.shape[1]
    half = per_block // 2
    row, me = lax.axis_index("row"), lax.axis_index("col")
    core = row % 2
    mate = row + 1 - 2 * core
    across = (row + 2) % 4
    peers = [partner(me, code) for code in CODES]

    def load(index):
        return pltpu.make_async_copy(
            weight.at[pl.ds(pl.multiple_of(index * per_block, per_block), per_block), :], deq.at[index], load_sem.at[index]
        )

    def start_load(index, carry):
        load(partner(me, code_at(index))).start()
        return carry

    lax.fori_loop(0, NCOL, start_load, 0)

    barrier = pltpu.get_barrier_semaphore()
    for peer in peers:
        pl.semaphore_signal(barrier, inc=1, device_id=(row, peer), device_id_type=MESH)
    for other in (1, 2, 3):
        pl.semaphore_signal(barrier, inc=1, device_id=((row + other) % 4, me), device_id_type=MESH)

    factor_top[...] = jnp.zeros(factor_top.shape, BF16)
    factor_bot[...] = jnp.zeros(factor_bot.shape, BF16)
    turned = sketch[...]
    factor_top[0:RANK, :] = turned
    factor_bot[RANK : 2 * RANK, :] = turned

    levels = [codebook[k] for k in range(LEVELS)]
    middles = []
    for k in range(LEVELS - 1):
        middle = (levels[k] + levels[k + 1]) * 0.5
        middles.append(middle + jnp.abs(middle) * 2.0**-21)

    pl.semaphore_wait(barrier, len(peers) + 3)

    def send_rows(peer, first, count, sem=None):
        rows = slice(first, first + count)
        copy = pltpu.make_async_remote_copy(
            src_ref=deq.at[peer, rows], dst_ref=quant.at[rows, pl.ds(pl.multiple_of(me * cols, 128), cols)],
            send_sem=block_sem.at[0] if sem is None else sem, recv_sem=block_sem.at[1],
            device_id=(row, peer), device_id_type=MESH,
        )
        copy.start()
        return copy

    def send_scales(peer):
        pltpu.make_async_remote_copy(
            src_ref=scale_out.at[peer], dst_ref=scale_in.at[me],
            send_sem=scale_sem.at[0], recv_sem=scale_sem.at[1], device_id=(row, peer), device_id_type=MESH,
        ).start()

    lane = lax.broadcasted_iota(jnp.int32, (16, 128), 1)

    def quantize_block(place, carry):
        block = partner(me, code_at(place))
        load(block).wait()

        def quantize_rows(group, inner):
            rows = pl.ds(pl.multiple_of(group * 16, 16), 16)
            shift = group // 2 * 32
            gathered = jnp.zeros((16, 128), F32)
            for tile in range(tiles):
                columns = slice(tile * 128, tile * 128 + 128)
                value = deq[block, rows, columns].astype(F32)
                size = jnp.abs(value)
                left = jnp.max(jnp.where(lane < BLOCK, size, 0.0), axis=1, keepdims=True)
                right = jnp.max(jnp.where(lane < BLOCK, 0.0, size), axis=1, keepdims=True)
                gathered = jnp.where(lane == shift + 2 * tile, left, gathered)
                gathered = jnp.where(lane == shift + 2 * tile + 1, right, gathered)
                spread = jnp.where(lane < BLOCK, left, right)
                unit_value = value * (1.0 / spread)
                level = jnp.full((16, 128), levels[0], F32)
                for k in range(LEVELS - 1):
                    level = jnp.where(unit_value > middles[k], levels[k + 1], level)
                dequant = level * spread
                deq[block, rows, columns] = dequant.astype(BF16)
                res[block, group // 3, pl.ds(pl.multiple_of(group % 3 * 16, 16), 16), columns] = (value - dequant).astype(BF16)
            held = pl.ds(pl.multiple_of(group % 2 * 16, 16), 16)
            before = scale_out[block, held, :].astype(F32)
            scale_out[block, held, :] = jnp.where(lane < shift, before, gathered).astype(BF16)
            return inner

        lax.fori_loop(0, per_block // 16, quantize_rows, 0)

        @pl.when((place % SPACING == 1) & (place // SPACING < EARLY))
        def _():
            for member in range(2):
                peer = partner(me, code_at(place // SPACING * 2 + member))
                send_rows(peer, 0, per_block)
                send_scales(peer)

        return carry

    scale_out[...] = jnp.zeros(scale_out.shape, BF16)
    lax.fori_loop(0, NCOL, quantize_block, 0)

    own = [
        pltpu.make_async_copy(deq.at[me], quant.at[:, pl.ds(pl.multiple_of(me * cols, 128), cols)], own_sem.at[0]),
        pltpu.make_async_copy(scale_out.at[me], scale_in.at[me], own_sem.at[1]),
    ]

    rounds, place = [], 0
    for group in ROUNDS:
        rounds.append(peers[place : place + len(group)])
        place += len(group)
    rounds = rounds[EARLY:]
    pieces = [(group, cut) for group in rounds for cut in range(CUTS)]
    state = {"sent": 0, "point": 0}

    def breathe():
        count = PACE[state["point"]]
        state["point"] += 1
        for group, cut in pieces[state["sent"] : state["sent"] + count]:
            for peer in group:
                send_rows(peer, cut * (per_block // CUTS), per_block // CUTS)
                if cut == 0:
                    send_scales(peer)
        state["sent"] += count

    rest = []

    def begin_rest():
        for group, cut in pieces[state["sent"] :]:
            rest.extend((peer, cut) for peer in group)
        for peer, cut in rest:
            if cut == 0:
                send_scales(peer)
        tail.extend(send_tail(place) for place in range(min(WINDOW, len(rest))))

    tail = []

    def send_tail(place):
        peer, cut = rest[place]
        return send_rows(peer, cut * (per_block // CUTS), per_block // CUTS, tail_sem.at[place % WINDOW])

    def end_rest():
        for place in range(WINDOW, len(rest)):
            tail[place - WINDOW].wait_send()
            tail.append(send_tail(place))

    def place_scales():
        width = scales.shape[1] // NCOL
        lanes = lax.broadcasted_iota(jnp.int32, (32, 128), 1)
        for group in range(per_block // 32):
            rows = slice(32 * group, 32 * group + 32)
            found = [jnp.zeros((32, 128), F32) for _ in range(scales.shape[1] // 128 + 1)]
            for source in range(NCOL):
                start = source * width
                tile, first = start // 128, start % 128
                turned = pltpu.roll(scale_in[source].astype(F32), (first - 32 * group) % 128, 1)
                found[tile] = jnp.where((lanes >= first) & (lanes < first + width), turned, found[tile])
                if first + width > 128:
                    found[tile + 1] = jnp.where(lanes < first + width - 128, turned, found[tile + 1])
            for tile, part in enumerate(found):
                left = min(128, scales.shape[1] - 128 * tile)
                if left > 0:
                    scales[rows, 128 * tile : 128 * tile + left] = part[:, :left]

    def sample(step):
        breathe()
        def some(turn, carry):
            part = (me // 8 + turn + 1) % 4
            blocks = pl.ds(pl.multiple_of(part * 8, 8), 8)
            top = res[blocks, 0].reshape(8 * half, cols)
            bottom = res[blocks, 1].reshape(8 * half, cols)
            both = dot_nt(top, factor_top[...]) + dot_nt(bottom, factor_bot[...])
            both = both[:, 0:128] + both[:, 128:256]
            sample_out[blocks] = both.reshape(8, half, 128).astype(BF16)
            for near in range(7, -1, -1):
                peer = part * 8 + (me // 4 + near // 4) % 2 * 4 + (me + near) % 4

                @pl.when(peer != me)
                def _():
                    pltpu.make_async_remote_copy(
                        src_ref=sample_out.at[peer], dst_ref=reduce_in.at[step, me],
                        send_sem=reduce_sem.at[step, 0], recv_sem=reduce_sem.at[step, 1],
                        device_id=(row, peer), device_id_type=MESH,
                    ).start()

            return carry

        lax.fori_loop(0, NCOL // 8, some, 0)
        reduce_in[step, pl.ds(me, 1)] = sample_out[pl.ds(me, 1)]
        breathe()
        drain(reduce_in.at[step, 0 : NCOL - 1], reduce_sem.at[step, 1])
        mine = jnp.sum(reduce_in[step].astype(F32), axis=0)
        gather_in[step, pl.ds(me, 1)] = mine.astype(BF16)[None]
        for peer in peers:
            pltpu.make_async_remote_copy(
                src_ref=gather_in.at[step, me], dst_ref=gather_in.at[step, me],
                send_sem=gather_sem.at[step, 0], recv_sem=gather_sem.at[step, 1], device_id=(row, peer), device_id_type=MESH,
            ).start()
        breathe()
        drain(reduce_in.at[step, 0 : NCOL - 1], reduce_sem.at[step, 0])
        drain(gather_in.at[step, 0 : NCOL - 1], gather_sem.at[step, 1])

    def begin_gram(step):
        packed = gather_in[step].reshape(NCOL * half, 128)
        sample_t[...] = packed.astype(F32).T.astype(BF16)
        gram = dot(sample_t[...], packed)
        gram = gram[0:RANK] + pltpu.roll(gram[RANK : 2 * RANK], RANK, 1)
        gram_out[step] = gram
        gram_in[step, pl.ds(row, 1)] = gram[None]
        for other in (1, 2, 3):
            pltpu.make_async_remote_copy(
                src_ref=gram_out.at[step], dst_ref=gram_in.at[step, row],
                send_sem=gram_sem.at[step, 0], recv_sem=gram_sem.at[step, 1],
                device_id=((row + other) % 4, me), device_id_type=MESH,
            ).start()

    def end_gram(step):
        drain(gram_in.at[step, 0:3], gram_sem.at[step, 1])
        drain(gram_in.at[step, 0:3], gram_sem.at[step, 0])
        gram = (gram_in[step, 0] + gram_in[step, 1]) + (gram_in[step, 2] + gram_in[step, 3])
        lanes = lax.broadcasted_iota(jnp.int32, (RANK, 128), 1)
        subs = lax.broadcasted_iota(jnp.int32, (RANK, 128), 0)
        work[...] = jnp.where(lanes < RANK, gram, jnp.where(lanes - RANK == subs, 1.0, 0.0))

    def eliminate(first, last):
        lanes = lax.broadcasted_iota(jnp.int32, (RANK, 128), 1)
        subs = lax.broadcasted_iota(jnp.int32, (RANK, 1), 0)

        def pivot(k, carry):
            held = work[...]
            line = work[pl.ds(k, 1), :]
            column = jnp.sum(jnp.where(lanes == k, held, 0.0), axis=1, keepdims=True)
            top = jnp.sum(jnp.where(lanes[0:1] == k, line, 0.0), axis=1, keepdims=True)
            scaled = jnp.where(subs > k, column, 0.0) * (1.0 / top)
            work[...] = held - scaled * line
            return carry

        lax.fori_loop(first, last, pivot, 0)

    def inverse_factor():
        lanes = lax.broadcasted_iota(jnp.int32, (RANK, 128), 1)
        subs = lax.broadcasted_iota(jnp.int32, (RANK, 128), 0)
        held = work[...]
        pivots = jnp.sum(jnp.where(lanes == subs, held, 0.0), axis=1, keepdims=True)
        return jnp.where(lanes < RANK, 0.0, held * (1.0 / jnp.sqrt(pivots)))

    def project_all(step):
        breathe()
        project[...] = jnp.zeros(project.shape, F32)

        def some(part, carry):
            blocks = pl.ds(pl.multiple_of(part * 16, 16), 16)
            depth = pl.ds(pl.multiple_of(part * 16 * half, 128), 16 * half)
            top = res[blocks, 0].reshape(16 * half, cols)
            bottom = res[blocks, 1].reshape(16 * half, cols)
            project[...] += dot(sample_t[0:RANK, depth], top) + dot(sample_t[RANK : 2 * RANK, depth], bottom)
            return carry

        lax.fori_loop(0, NCOL // 16, some, 0)

    def reduce_project(step):
        part = RANK // 2
        mine = pl.ds(pl.multiple_of(core * part, part), part)
        other = pl.ds(pl.multiple_of((1 - core) * part, part), part)
        one = pltpu.make_async_remote_copy(
            src_ref=project.at[other, :], dst_ref=half_in.at[step],
            send_sem=half_sem.at[step, 0], recv_sem=half_sem.at[step, 1], device_id=(mate, me), device_id_type=MESH,
        )
        one.start()
        breathe()
        end_gram(step)
        one.wait()
        sent, met = (pair_out, pair_in.at[step]) if step < POWER else (last_out, last_in)
        sent[...] = (project[mine, :] + half_in[step]).astype(sent.dtype)
        two = pltpu.make_async_remote_copy(
            src_ref=sent, dst_ref=met,
            send_sem=pair_sem.at[step, 0], recv_sem=pair_sem.at[step, 1], device_id=(across, me), device_id_type=MESH,
        )
        two.start()
        breathe()
        eliminate(0, RANK // 2)
        two.wait()
        total[step, mine, :] = sent[...].astype(F32) + met[...].astype(F32)
        three = pltpu.make_async_remote_copy(
            src_ref=total.at[step, mine, :], dst_ref=total.at[step, mine, :],
            send_sem=total_sem.at[step, 0], recv_sem=total_sem.at[step, 1], device_id=(mate, me), device_id_type=MESH,
        )
        three.start()
        breathe()
        eliminate(RANK // 2, RANK)
        three.wait()

    root = math.sqrt(ROWS)
    for step in range(POWER + 1):
        sample(step)
        if step == 0:
            for copy in own:
                copy.start()
        begin_gram(step)
        project_all(step)
        reduce_project(step)
        inverse = inverse_factor()
        factor = dot(pltpu.roll(inverse, RANK, 1)[:, 0:RANK], total[step], HIGH)
        if step < POWER:
            upper = factor.astype(BF16)
            lower = (factor - upper.astype(F32)).astype(BF16)
            factor_top[0:RANK, :] = upper
            factor_top[2 * RANK : 3 * RANK, :] = lower
            factor_bot[RANK : 2 * RANK, :] = upper
            factor_bot[3 * RANK : 4 * RANK, :] = lower
        else:
            begin_rest()
            lora_b[...] = factor * (1.0 / root)
            packed = gather_in[step].reshape(NCOL * half, 128).astype(F32)
            right = inverse * root
            left = pltpu.roll(right, RANK, 1)
            basis[:, 0] = dot_nt(packed, left, HIGH).reshape(NCOL, half, RANK)
            basis[:, 1] = dot_nt(packed, right, HIGH).reshape(NCOL, half, RANK)
            lora_a[...] = basis[...].reshape(lora_a.shape[1], RANK).T
        drain(gather_in.at[step, 0 : NCOL - 1], gather_sem.at[step, 0])
    end_rest()
    for copy in own:
        copy.wait()
    drain(scale_out.at[0 : NCOL - 1], scale_sem.at[0])
    drain(scale_in.at[0 : NCOL - 1], scale_sem.at[1])
    place_scales()
    for copy in tail[-WINDOW:]:
        copy.wait_send()
    apart = len(rest) * (per_block // CUTS)
    whole, over = divmod((NCOL - 1) * per_block - apart, per_block)
    drain(deq.at[0:whole], block_sem.at[0])
    if over:
        drain(deq.at[0, 0:over], block_sem.at[0])
    drain(quant.at[:, pl.ds(0, (NCOL - 1) * cols)], block_sem.at[1])


def finish(*refs):
    count = len(refs) // 3
    sources, targets, held, (load_sem, store_sem) = refs[:count], refs[count : 2 * count], refs[2 * count : 3 * count], refs[3 * count :]
    strips = [(0, slice(16 * k, 16 * k + 16)) for k in range(sources[0].shape[0] // 16)]
    strips += [(k, slice(0, sources[k].shape[0])) for k in range(1, count)]
    loads, stores = [], []
    for place, (k, rows) in enumerate(strips):
        loads.append(pltpu.make_async_copy(sources[k].at[rows], held[k].at[rows], load_sem.at[place]))
        stores.append(pltpu.make_async_copy(held[k].at[rows], targets[k].at[rows], store_sem.at[place]))
    for load in loads:
        load.start()
    for load, store in zip(loads, stores):
        load.wait()
        store.start()
    for store in stores:
        store.wait()


def body(weight, sketch, codebook):
    rows, cols = weight.shape
    per_block = rows // NCOL
    half = per_block // 2
    steps = POWER + 1
    anywhere = pl.BlockSpec(memory_space=pl.ANY)
    local = pl.BlockSpec(memory_space=pltpu.VMEM)
    dma = pltpu.SemaphoreType.DMA
    quant, scales, lora_a, lora_b = pl.pallas_call(
        kernel,
        name="loftq",
        out_shape=(
            jax.ShapeDtypeStruct((per_block, NCOL * cols), BF16),
            jax.ShapeDtypeStruct((per_block, NCOL * cols // BLOCK), F32),
            jax.ShapeDtypeStruct((RANK, rows), F32),
            jax.ShapeDtypeStruct((RANK, cols), F32),
        ),
        in_specs=[anywhere, local, pl.BlockSpec(memory_space=pltpu.SMEM)],
        out_specs=(anywhere, local, local, local),
        scratch_shapes=[
            pltpu.VMEM((NCOL, per_block, cols), BF16),
            pltpu.VMEM((NCOL, 2, half, cols), BF16),
            pltpu.VMEM((NCOL, 32, 128), BF16),
            pltpu.VMEM((NCOL, 32, 128), BF16),
            pltpu.VMEM((NCOL, 2, half, RANK), F32),
            pltpu.VMEM((4 * RANK, cols), BF16),
            pltpu.VMEM((4 * RANK, cols), BF16),
            pltpu.VMEM((NCOL, half, 128), BF16),
            pltpu.VMEM((steps, NCOL, half, 128), BF16),
            pltpu.VMEM((steps, NCOL, half, 128), BF16),
            pltpu.VMEM((128, NCOL * half), BF16),
            pltpu.VMEM((RANK, cols), F32),
            pltpu.VMEM((steps, RANK // 2, cols), F32),
            pltpu.VMEM((RANK // 2, cols), BF16),
            pltpu.VMEM((POWER, RANK // 2, cols), BF16),
            pltpu.VMEM((RANK // 2, cols), F32),
            pltpu.VMEM((RANK // 2, cols), F32),
            pltpu.VMEM((steps, RANK, cols), F32),
            pltpu.VMEM((steps, 4, RANK, 128), F32),
            pltpu.VMEM((steps, RANK, 128), F32),
            pltpu.VMEM((RANK, 128), F32),
            dma((NCOL,)),
            dma((2,)),
            dma((2,)),
            dma((2,)),
            dma((steps, 2)),
            dma((steps, 2)),
            dma((steps, 2)),
            dma((steps, 2)),
            dma((steps, 2)),
            dma((steps, 2)),
            dma((WINDOW,)),
        ],
        compiler_params=pltpu.CompilerParams(
            collective_id=0, has_side_effects=True, vmem_limit_bytes=56 * 1024 * 1024
        ),
    )(weight, sketch.T, codebook.astype(F32))
    results = [quant, scales, lora_a, lora_b]
    quant, scales, lora_a, lora_b = pl.pallas_call(
        finish,
        name="finish",
        out_shape=tuple(jax.ShapeDtypeStruct(result.shape, result.dtype) for result in results),
        in_specs=[anywhere] * 4,
        out_specs=(anywhere,) * 4,
        scratch_shapes=[pltpu.VMEM(result.shape, result.dtype) for result in results]
        + [dma((per_block // 16 + 3,)), dma((per_block // 16 + 3,))],
        compiler_params=pltpu.CompilerParams(vmem_limit_bytes=58 * 1024 * 1024),
    )(*results)
    return quant, scales, lora_a.T, lora_b


def solution(mesh):
    in_specs = (P("row", "col"), P("col", None), P())
    out_specs = (P(("row", "col"), None), P(("row", "col"), None), P("row", None), P(None, "col"))
    return jax.shard_map(body, mesh=mesh, in_specs=in_specs, out_specs=out_specs, check_vma=False)
```
